32 devices in a mesh: grp: 2 (over y), seq: 8 (over z, x), fsdp: 2 (over core).
Axes of the slice: x: 2, y: 2, z: 4, core: 2. Of those that a mesh axis runs over, the one named last changes fastest.
Arguments:
- base_codes: int32 [4, 4096], P(('grp', 'fsdp'), 'seq'), parts along dimension 0, may hold values from 0 to 3
- stem_weight: bfloat16 [15, 4, 1536], replicated, may hold values from -1.5 to 1.5
- norm_gains: float32 [2, 1536], replicated, may hold values from 0.1 to 1.9
- conv_weight: bfloat16 [2, 1536, 3, 384], P(None, 'fsdp'), may hold values from -0.09375 to 0.09375
- point_weight: bfloat16 [2, 1536, 384], P(None, 'fsdp'), may hold values from -0.3125 to 0.3125
- cotangent: bfloat16 [4, 1536, 2048], P(('grp', 'fsdp'), 'seq'), parts along dimension 0, may hold values from -0.29882812 to 0.29882812
Outputs:
- pooled: bfloat16 [4, 1536, 2048], P(('grp', 'fsdp'), 'seq'), parts along dimension 0
- saliency: float32 [4, 4, 4096], P(('grp', 'fsdp'), None, 'seq'), parts along dimension 0
The draws below stay inside these ranges and needn't reach their ends.
There are 2 independent parts, one for each index of `grp`. The reference program is written for one: setup_inputs(seed, part) draws one part's arguments, and reference() takes and returns one part's arrays. A program takes and returns all parts, laid end to end along the dimension named above; an argument that names none is the same for every part. Nothing has to cross between parts.
Inputs may be any that keep to these rules, and one draw needn't show every extreme that they name: `base_codes`: codes of the bases A, C, G and T.
All inputs are finite; a program needn't handle non-finite values.
Results may differ from the reference program's by a relative error of at most 0.0055.
Values may be sent and summed in bfloat16 or wider, within the bound.
A program may use at most 128 MiB of HBM per device.

```python
import jax
import jax.numpy as jnp
from jax import lax

C = 1536
FF = 384
KW = 3
STEM = 15
BASES = 4
FIRST_DILATION = 32
LAYERS = 2
POOL = 2
BATCH = 2
LENGTH = 4096
POOLED = 2048


def with_ends(result, rng, low, top_value):
    spot = [jax.random.randint(jax.random.fold_in(rng, axis), (), 0, length) for axis, length in enumerate(result.shape)]
    longest = result.shape.index(max(result.shape))
    neighbour = spot[:longest] + [(spot[longest] + 1) % result.shape[longest]] + spot[longest + 1:]
    return result.at[tuple(spot)].set(low).at[tuple(neighbour)].set(top_value)


def block_levels(own_key, shape, pieces, low, largest):
    def one(position, blocks):
        steps = jax.random.uniform(jax.random.fold_in(jax.random.fold_in(own_key, 6), position), (blocks,), jnp.float32, low / len(pieces), largest / len(pieces))
        return jnp.repeat(jnp.exp(steps), shape[position] // blocks).reshape((-1,) + (1,) * (len(shape) - position - 1))

    level = one(*pieces[0])
    for cut in pieces[1:]:
        level = level * one(*cut)
    return level


def noise(key, extent, width, most, pieces=(), held_as=jnp.bfloat16):
    values = width * jax.random.normal(key, extent, jnp.float32)
    if pieces:
        values = values * block_levels(key, extent, pieces, -0.22, 0.18)
    return jnp.clip(values, -most, most).astype(held_as)


def setup_inputs(seed: int = 0, part: int = 0) -> dict:
    key_of = jax.random.split(jax.random.key(seed), 7)
    part_splits = jax.random.split(jax.random.fold_in(key_of[6], part), 7)
    return {
        "base_codes": with_ends(jax.random.randint(part_splits[0], (BATCH, LENGTH), 0, BASES), jax.random.fold_in(part_splits[0], 1), 0, BASES - 1).astype(jnp.int32),
        "stem_weight": noise(key_of[1], (STEM, BASES, C), STEM ** -0.5, 1.5),
        "norm_gains": jnp.clip(1.0 + 0.18 * jax.random.normal(key_of[2], (LAYERS, C), jnp.float32), 0.1, 1.9),
        "conv_weight": noise(key_of[3], (LAYERS, C, KW, FF), (C * KW) ** -0.5, 0.09375, ((1, 2),)),
        "point_weight": noise(key_of[4], (LAYERS, C, FF), FF ** -0.5, 0.3125, ((1, 2),)),
        "cotangent": noise(part_splits[5], (BATCH, C, POOLED), 0.05, 0.29882812, ((0, 2), (1, 8))),
    }


def rms_gain(hidden, gain_row):
    inv_rms = lax.rsqrt(lax.optimization_barrier(jnp.mean(hidden * hidden, axis=-1, keepdims=True)) + 1e-06)
    return hidden * inv_rms * gain_row

def activate(hidden, gain_row):
    return jax.nn.gelu(rms_gain(hidden, gain_row))

def through_norm(hidden, gain_row, gradient):
    _, pullback = jax.vjp(lambda inputs: activate(inputs, gain_row), hidden)
    return pullback(gradient)[0]

def through_gelu(conv_out, gradient):
    _, pullback = jax.vjp(jax.nn.gelu, conv_out)
    return pullback(gradient)[0]

def shifted_sum(source, weights, dilation_rate, forward):
    tap_count = weights.shape[1]
    half_span = tap_count // 2 * dilation_rate
    length_rows = source.shape[0]
    padded = jnp.pad(source, ((half_span, half_span), (0, 0)))
    summed = None
    for tap_index in range(tap_count):
        if forward:
            first_row = tap_index * dilation_rate
            window = padded[first_row:first_row + length_rows]
            term = jnp.dot(window, weights[:, tap_index, :], preferred_element_type=jnp.float32)
        else:
            first_row = (tap_count - 1 - tap_index) * dilation_rate
            window = padded[first_row:first_row + length_rows]
            term = jnp.dot(window, weights[:, tap_index, :].T, preferred_element_type=jnp.float32)
        summed = term if summed is None else summed + term
    return summed

def stem_forward(sequence_codes, stem_weight):
    stem_half = STEM // 2
    onehot = (sequence_codes[:, None] == jnp.arange(BASES, dtype=jnp.int32)[None, :]).astype(jnp.bfloat16)
    padded = jnp.pad(onehot, ((stem_half, stem_half), (0, 0)))
    stacked = jnp.concatenate([padded[tap_index:tap_index + LENGTH] for tap_index in range(STEM)], axis=1)
    return jnp.dot(stacked, stem_weight.reshape(STEM * BASES, C), preferred_element_type=jnp.float32)

def stem_backward(gradient, stem_weight):
    stem_half = STEM // 2
    stem_flat = stem_weight.reshape(STEM * BASES, C).astype(jnp.float32)
    output_projection = jnp.dot(stem_flat, gradient.T, precision=lax.Precision.HIGHEST)
    padded = jnp.pad(output_projection, ((0, 0), (stem_half, stem_half))).reshape(STEM, BASES, LENGTH + 2 * stem_half)
    saliency = None
    for tap_index in range(STEM):
        first_col = STEM - 1 - tap_index
        term = padded[tap_index, :, first_col:first_col + LENGTH]
        saliency = term if saliency is None else saliency + term
    return saliency

def one_sequence(sequence_codes, stem_weight, norm_gains, conv_weight, point_weight, cotangent):
    hidden = stem_forward(sequence_codes, stem_weight)
    stored = []
    for layer_number_index in range(LAYERS):
        dilation_rate = FIRST_DILATION * 2 ** layer_number_index
        activation = activate(hidden, norm_gains[layer_number_index]).astype(jnp.bfloat16)
        conv_out = shifted_sum(activation, conv_weight[layer_number_index], dilation_rate, True)
        bottleneck = jax.nn.gelu(conv_out).astype(jnp.bfloat16)
        stored.append((hidden, conv_out))
        hidden = hidden + jnp.dot(bottleneck, point_weight[layer_number_index].T, preferred_element_type=jnp.float32)
    pooled = lax.optimization_barrier(jnp.mean(hidden.reshape(LENGTH // POOL, POOL, C), axis=1)).T.astype(jnp.bfloat16)
    spread = cotangent.astype(jnp.float32).T / POOL
    gradient = jnp.broadcast_to(spread[:, None, :], (LENGTH // POOL, POOL, C)).reshape(LENGTH, C)
    for layer_number_index in reversed(range(LAYERS)):
        dilation_rate = FIRST_DILATION * 2 ** layer_number_index
        start_hidden, conv_out = stored[layer_number_index]
        bottleneck_gradient = jnp.dot(gradient.astype(jnp.bfloat16), point_weight[layer_number_index], preferred_element_type=jnp.float32)
        convolution_gradient = through_gelu(conv_out, bottleneck_gradient).astype(jnp.bfloat16)
        grad_activation = shifted_sum(convolution_gradient, conv_weight[layer_number_index], dilation_rate, False)
        gradient = gradient + through_norm(start_hidden, norm_gains[layer_number_index], grad_activation)
    saliency = stem_backward(gradient, stem_weight)
    return (pooled, saliency)

def reference(base_codes, stem_weight, norm_gains, conv_weight, point_weight, cotangent):
    pooled_list = []
    saliency_list = []
    for sequence_index in range(BATCH):
        pooled_one, saliency_one = one_sequence(base_codes[sequence_index], stem_weight, norm_gains, conv_weight, point_weight, cotangent[sequence_index])
        pooled_list.append(pooled_one)
        saliency_list.append(saliency_one)
    return (jnp.stack(pooled_list), jnp.stack(saliency_list))
```

```python
import functools

import jax
import jax.numpy as jnp
from jax import lax
from jax.experimental import pallas as pl
from jax.experimental.pallas import tpu as pltpu
from jax.sharding import PartitionSpec as P

D0 = 32
D1 = 64
POOL = 2
EDGE = 128
GC = 0.7978845608028654
GA = 0.044715
F32 = jnp.float32
BF16 = jnp.bfloat16
MESH = pl.DeviceIdType.MESH


def nn(a, b):
    return lax.dot_general(a, b, (((1,), (0,)), ((), ())), preferred_element_type=F32)


def nt(a, b):
    return lax.dot_general(a, b, (((1,), (1,)), ((), ())), preferred_element_type=F32)


def gelu(x):
    return (0.5 * x) * (1.0 + jnp.tanh(x * (GC + (GC * GA) * (x * x))))


def gelu_slope(x):
    xx = x * x
    t = jnp.tanh(x * (GC + (GC * GA) * xx))
    return 0.5 * (1.0 + t) + (0.5 * x) * (1.0 - t * t) * (GC + (3.0 * GC * GA) * xx)


def kernel(n, codes, stem, gains, wconv, wpoint, cot, pooled_out, sal_out,
           wc, wp, oh, h0, act0, co0, h1, act1, co1, pool, sendp, recc, cott, grad, ga,
           gc1, gc0, glo, code_l, code_r, pj_l, pj_r, pj_s,
           wl_sem, ws_sem, wr_sem, cs_sem, cr_sem, ps_sem, pr_sem, own_sem,
           hs_sem, hr_sem):
    me = lax.axis_index("seq")
    f = lax.axis_index("fsdp")
    rows = codes.shape[1]
    ch = cot.shape[1]
    half = wpoint.shape[1]
    chan = 2 * half
    prow = rows // POOL
    layers = wpoint.shape[0]
    left, right = me - 1, me + 1
    has_left, has_right = me > 0, me < n - 1
    e0 = D0 + D1

    def local_w():
        copies = []
        for l in range(layers):
            copies.append(pltpu.make_async_copy(wconv.at[l], wc.at[l, :, pl.ds(pl.multiple_of(f * half, half), half), :], wl_sem.at[2 * l]))
            copies.append(pltpu.make_async_copy(wpoint.at[l], wp.at[l, pl.ds(pl.multiple_of(f * half, half), half), :], wl_sem.at[2 * l + 1]))
        return copies

    def remote_w():
        copies = []
        for l in range(layers):
            copies.append(pltpu.make_async_remote_copy(
                wconv.at[l], wc.at[l, :, pl.ds(pl.multiple_of(f * half, half), half), :],
                ws_sem.at[2 * l], wr_sem.at[2 * l], device_id={"fsdp": 1 - f}, device_id_type=MESH))
            copies.append(pltpu.make_async_remote_copy(
                wpoint.at[l], wp.at[l, pl.ds(pl.multiple_of(f * half, half), half), :],
                ws_sem.at[2 * l + 1], wr_sem.at[2 * l + 1], device_id={"fsdp": 1 - f}, device_id_type=MESH))
        return copies

    own_w, sib_w = local_w(), remote_w()
    for c in own_w:
        c.start()

    barrier = pltpu.get_barrier_semaphore()

    @pl.loop(1, n)
    def _(i):
        pl.semaphore_signal(barrier, inc=1, device_id={"seq": lax.rem(me + i, n)}, device_id_type=MESH)

    pl.semaphore_signal(barrier, inc=1, device_id={"fsdp": 1 - f}, device_id_type=MESH)
    pl.semaphore_wait(barrier, n)

    def edge(k, to_left_src, to_left_dst, to_right_src, to_right_dst):
        tl = pltpu.make_async_remote_copy(to_left_src, to_left_dst, hs_sem.at[2 * k], hr_sem.at[2 * k],
                                          device_id={"seq": left}, device_id_type=MESH)
        tr = pltpu.make_async_remote_copy(to_right_src, to_right_dst, hs_sem.at[2 * k + 1], hr_sem.at[2 * k + 1],
                                          device_id={"seq": right}, device_id_type=MESH)

        def start():
            pl.when(has_left)(lambda: tl.start())
            pl.when(has_right)(lambda: tr.start())

        def recv():
            pl.when(has_right)(lambda: tl.wait_recv())
            pl.when(has_left)(lambda: tr.wait_recv())

        def sent():
            pl.when(has_left)(lambda: tl.wait_send())
            pl.when(has_right)(lambda: tr.wait_send())

        return start, recv, sent

    codes_x = edge(0, codes.at[:, pl.ds(0, EDGE)], code_r, codes.at[:, pl.ds(rows - EDGE, EDGE)], code_l)
    codes_x[0]()
    sib_w[0].start()
    sib_w[1].start()

    def cot_copy(i, slot):
        peer = lax.rem(me + i, n)
        return pltpu.make_async_remote_copy(
            cot.at[0, :, pl.ds(pl.multiple_of(peer * prow, 128), prow)], recc.at[slot],
            cs_sem.at[i], cr_sem.at[i], device_id={"seq": peer}, device_id_type=MESH)

    cot_own = pltpu.make_async_copy(cot.at[0, :, pl.ds(pl.multiple_of(me * prow, 128), prow)], recc.at[me], own_sem.at[0])
    cot_own.start()

    @pl.loop(1, n)
    def _(i):
        cot_copy(i, me).start()

    sib_w[2].start()
    sib_w[3].start()

    @pl.when(jnp.logical_not(has_left))
    def _():
        code_l[...] = jnp.full(code_l.shape, -1, jnp.int32)
        gc1[pl.ds(0, D1), :] = jnp.zeros((D1, gc1.shape[1]), BF16)
        gc0[pl.ds(0, D0), :] = jnp.zeros((D0, gc0.shape[1]), BF16)
        pj_l[...] = jnp.zeros(pj_l.shape, BF16)

    @pl.when(jnp.logical_not(has_right))
    def _():
        code_r[...] = jnp.full(code_r.shape, -1, jnp.int32)
        gc1[pl.ds(D1 + rows, D1), :] = jnp.zeros((D1, gc1.shape[1]), BF16)
        gc0[pl.ds(D0 + rows, D0), :] = jnp.zeros((D0, gc0.shape[1]), BF16)
        pj_r[...] = jnp.zeros(pj_r.shape, BF16)

    codes_x[1]()

    wide = rows + 2 * EDGE
    ext = jnp.concatenate([code_l[...], codes[...], code_r[...]], axis=1)
    ext = jnp.broadcast_to(ext, (8, wide))
    sub = lax.broadcasted_iota(jnp.int32, (8, wide), 0)
    low_half = sub < 4
    base = jnp.where(low_half, sub, sub - 4)
    groups = []
    off = EDGE - e0 - 7
    for j in range(8):
        a = pltpu.roll(ext, wide - (off + 2 * j), 1)
        b = pltpu.roll(ext, wide - (off + 2 * j + 1), 1)
        groups.append(jnp.where(jnp.where(low_half, a, b) == base, 1.0, 0.0).astype(F32))
    oh[...] = jnp.concatenate(groups, axis=0).T.astype(BF16)

    ext0 = rows + 2 * e0
    hb = ext0 // 4

    @pl.loop(0, 4)
    def _(b):
        s = pl.multiple_of(b * hb, 16)
        h0[pl.ds(s, hb), :] = nn(oh[pl.ds(s, hb), :], stem[...])

    def activate(src, dst, count, halo, layer):
        gain = gains[pl.ds(layer, 1), :]

        @pl.loop(0, count // 16, unroll=2)
        def _(b):
            s = pl.multiple_of(b * 16, 16)
            x = src[pl.ds(s, 16), :]
            r = lax.rsqrt(jnp.sum(x * x, axis=1, keepdims=True) * (1.0 / chan) + 1e-06)
            pos = me * rows - halo + s + lax.broadcasted_iota(jnp.int32, (16, 1), 0)
            keep = jnp.where((pos >= 0) & (pos < n * rows), 1.0, 0.0)
            dst[pl.ds(s, 16), :] = (gelu(x * r * gain) * keep).astype(BF16)

    activate(h0, act0, ext0, e0, 0)

    own_w[0].wait()
    sib_w[0].wait_recv()
    own_w[1].wait()
    sib_w[1].wait_recv()

    def taps(ref, start, count, d, order):
        return jnp.concatenate([ref[pl.ds(pl.multiple_of(start + k * d, 32), count), :] for k in order], axis=1)

    ext1 = rows + 2 * D1
    b1 = ext1 // 2
    flat = (3 * chan, wc.shape[3])

    @pl.loop(0, 2)
    def _(b):
        s = pl.multiple_of(b * b1, 64)
        c = nn(taps(act0, s, b1, D0, (0, 1, 2)), wc[0].reshape(flat))
        co0[pl.ds(s, b1), :] = c
        h1[pl.ds(s, b1), :] = h0[pl.ds(pl.multiple_of(s + D0, 32), b1), :] + nt(gelu(c).astype(BF16), wp[0])

    activate(h1, act1, ext1, D1, 1)

    own_w[2].wait()
    sib_w[2].wait_recv()
    own_w[3].wait()
    sib_w[3].wait_recv()

    b2 = rows // 2
    pb = b2 // POOL
    pr = lax.broadcasted_iota(jnp.int32, (pb, b2), 0)
    pc = lax.broadcasted_iota(jnp.int32, (pb, b2), 1)
    pool_mat = jnp.where((pc == 2 * pr) | (pc == 2 * pr + 1), 0.5, 0.0).astype(BF16)

    @pl.loop(0, 2)
    def _(b):
        s = pl.multiple_of(b * b2, 64)
        c = nn(taps(act1, s, b2, D1, (0, 1, 2)), wc[1].reshape(flat))
        co1[pl.ds(s, b2), :] = c
        h2 = h1[pl.ds(pl.multiple_of(s + D1, 64), b2), :] + nt(gelu(c).astype(BF16), wp[1])
        hi = h2.astype(BF16)
        lo = (h2 - hi.astype(F32)).astype(BF16)
        pool[pl.ds(pl.multiple_of(b * pb, 64), pb), :] = nn(pool_mat, hi) + nn(pool_mat, lo)

    sendp[...] = pool[...].T.reshape(n, ch, prow).astype(BF16)

    def pool_copy(i, slot):
        peer = lax.rem(me + i, n)
        return pltpu.make_async_remote_copy(
            sendp.at[peer], pooled_out.at[0, :, pl.ds(pl.multiple_of(slot * prow, 128), prow)],
            ps_sem.at[i], pr_sem.at[i], device_id={"seq": peer}, device_id_type=MESH)

    pool_own = pltpu.make_async_copy(sendp.at[me], pooled_out.at[0, :, pl.ds(pl.multiple_of(me * prow, 128), prow)], own_sem.at[1])
    pool_own.start()

    @pl.loop(1, n)
    def _(i):
        pool_copy(i, me).start()

    cot_own.wait()

    @pl.loop(1, n)
    def _(i):
        cot_copy(i, lax.rem(me + n - i, n)).wait_recv()

    cott[...] = recc[...].astype(F32).reshape(chan, prow).astype(BF16)
    er = lax.broadcasted_iota(jnp.int32, (b2, pb), 0)
    ec = lax.broadcasted_iota(jnp.int32, (b2, pb), 1)
    spread = jnp.where((er == 2 * ec) | (er == 2 * ec + 1), 0.5, 0.0).astype(BF16)

    @pl.loop(0, 2)
    def _(b):
        s = pl.multiple_of(b * b2, 64)
        g = nt(spread, cott[:, pl.ds(pl.multiple_of(b * pb, 128), pb)])
        grad[pl.ds(s, b2), :] = g
        gb = nn(g.astype(BF16), wp[1])
        gc1[pl.ds(pl.multiple_of(D1 + s, 64), b2), :] = (gb * gelu_slope(co1[pl.ds(s, b2), :])).astype(BF16)

    def back(x_edge, gc, d, layer, hidden, hoff, low):
        gain = gains[pl.ds(layer, 1), :]
        x_edge[1]()

        @pl.loop(0, 2)
        def _(b):
            s = pl.multiple_of(b * b2, 64)
            w = jnp.concatenate([wc[layer, 0], wc[layer, 1], wc[layer, 2]], axis=1)
            ga[pl.ds(s, b2), :] = nt(taps(gc, s, b2, d, (2, 1, 0)), w)

        @pl.loop(0, rows // 16, unroll=2)
        def _(b):
            s = pl.multiple_of(b * 16, 16)
            x = hidden[pl.ds(pl.multiple_of(s + hoff, 16), 16), :]
            r = lax.rsqrt(jnp.sum(x * x, axis=1, keepdims=True) * (1.0 / chan) + 1e-06)
            dn = ga[pl.ds(s, 16), :] * gelu_slope(x * r * gain) * gain
            m = jnp.sum(dn * x, axis=1, keepdims=True) * (r * r * r * (1.0 / chan))
            g = grad[pl.ds(s, 16), :] + (dn * r - x * m)
            if low is None:
                grad[pl.ds(s, 16), :] = g
            else:
                hi = g.astype(BF16)
                low[0, pl.ds(s, 16), :] = hi
                low[1, pl.ds(s, 16), :] = (g - hi.astype(F32)).astype(BF16)

    x1 = edge(1, gc1.at[pl.ds(D1, D1), :], gc1.at[pl.ds(D1 + rows, D1), :],
              gc1.at[pl.ds(rows, D1), :], gc1.at[pl.ds(0, D1), :])
    x1[0]()
    back(x1, gc1, D1, 1, h1, D1, None)

    @pl.loop(0, 2)
    def _(b):
        s = pl.multiple_of(b * b2, 64)
        gb = nn(grad[pl.ds(s, b2), :].astype(BF16), wp[0])
        gc0[pl.ds(pl.multiple_of(D0 + s, 32), b2), :] = (gb * gelu_slope(co0[pl.ds(pl.multiple_of(s + D1, 64), b2), :])).astype(BF16)

    x0 = edge(2, gc0.at[pl.ds(D0, D0), :], gc0.at[pl.ds(D0 + rows, D0), :],
              gc0.at[pl.ds(rows, D0), :], gc0.at[pl.ds(0, D0), :])
    x0[0]()
    back(x0, gc0, D0, 0, h0, e0, glo)

    proj = nt(stem[...], glo[0]) + nt(stem[...], glo[1])
    pj_s[0] = proj[:, 0:EDGE].astype(BF16)
    pj_s[1] = proj[:, rows - EDGE:rows].astype(BF16)
    xp = edge(3, pj_s.at[0], pj_r, pj_s.at[1], pj_l)
    xp[0]()
    xp[1]()
    full = jnp.concatenate([pj_l[...].astype(F32), proj, pj_r[...].astype(F32)], axis=1)
    total = jnp.zeros((8, wide), F32)
    for j in range(8):
        grp = full[8 * j:8 * j + 8, :]
        a = pltpu.roll(grp, (2 * j - 7) % wide, 1)
        b = pltpu.roll(grp, (2 * j - 6) % wide, 1)
        total = total + jnp.where(low_half, a, b)
    both = total + pltpu.roll(total, 4, 0)
    sal_out[0] = both[0:4, EDGE:EDGE + rows]

    pool_own.wait()

    @pl.loop(1, n)
    def _(i):
        cot_copy(i, me).wait_send()
        pool_copy(i, lax.rem(me + n - i, n)).wait_recv()
        pool_copy(i, me).wait_send()

    for c in sib_w:
        c.wait_send()
    for x in (codes_x, x1, x0, xp):
        x[2]()


def body(n, base_codes, stem_weight, norm_gains, conv_weight, point_weight, cotangent):
    rows = base_codes.shape[1]
    ch, prow = cotangent.shape[1], rows // POOL
    layers, half, taps_n, ff = conv_weight.shape
    chan = 2 * half
    taps_b = stem_weight.shape[0] * stem_weight.shape[1]
    stem = jnp.pad(stem_weight.reshape(taps_b, chan), ((0, 64 - taps_b), (0, 0)))
    wconv = conv_weight.transpose(0, 2, 1, 3)
    any_spec = pl.BlockSpec(memory_space=pl.ANY)
    vm = pl.BlockSpec(memory_space=pltpu.VMEM)
    ext0, ext1 = rows + 2 * (D0 + D1), rows + 2 * D1
    V = pltpu.VMEM
    DMA = pltpu.SemaphoreType.DMA
    return pl.pallas_call(
        functools.partial(kernel, n),
        out_shape=(jax.ShapeDtypeStruct(cotangent.shape, BF16),
                   jax.ShapeDtypeStruct((1, 4, rows), F32)),
        in_specs=[vm, vm, vm, any_spec, any_spec, any_spec],
        out_specs=(any_spec, vm),
        scratch_shapes=[
            V((layers, taps_n, chan, ff), BF16), V((layers, chan, ff), BF16),
            V((rows + 2 * EDGE, 64), BF16),
            V((ext0, chan), F32), V((ext0, chan), BF16), V((ext1, ff), F32),
            V((ext1, chan), F32), V((ext1, chan), BF16), V((rows, ff), F32),
            V((prow, chan), F32), V((n, ch, prow), BF16), V((n, ch, prow), BF16),
            V((chan, prow), BF16), V((rows, chan), F32), V((rows, chan), F32),
            V((ext1, ff), BF16), V((rows + 2 * D0, ff), BF16), V((2, rows, chan), BF16),
            V((1, EDGE), jnp.int32), V((1, EDGE), jnp.int32),
            V((64, EDGE), BF16), V((64, EDGE), BF16), V((2, 64, EDGE), BF16),
            DMA((2 * layers,)), DMA((2 * layers,)), DMA((2 * layers,)),
            DMA((n,)), DMA((n,)), DMA((n,)), DMA((n,)), DMA((2,)),
            DMA((8,)), DMA((8,)),
        ],
        compiler_params=pltpu.CompilerParams(
            collective_id=0, has_side_effects=True, vmem_limit_bytes=56 * 1024 * 1024),
        cost_estimate=pl.CostEstimate(flops=10_000_000_000, bytes_accessed=12_000_000, transcendentals=4_000_000),
    )(base_codes, stem, norm_gains, wconv, point_weight, cotangent)


def solution(mesh):
    in_specs = (
        P(("grp", "fsdp"), "seq"),
        P(),
        P(),
        P(None, "fsdp", None, None),
        P(None, "fsdp", None),
        P(("grp", "fsdp"), "seq", None),
    )
    out_specs = (P(("grp", "fsdp"), "seq", None), P(("grp", "fsdp"), None, "seq"))
    return jax.shard_map(functools.partial(body, mesh.shape["seq"]), mesh=mesh,
                         in_specs=in_specs, out_specs=out_specs, check_vma=False)
```

```python
import functools

import jax
import jax.numpy as jnp
from jax import lax
from jax.experimental import pallas as pl
from jax.experimental.pallas import tpu as pltpu
from jax.sharding import PartitionSpec as P

D0 = 32
D1 = 64
POOL = 2
EDGE = 128
GC = 0.7978845608028654
GA = 0.044715
F32 = jnp.float32
BF16 = jnp.bfloat16
MESH = pl.DeviceIdType.MESH


def nn(a, b):
    return lax.dot_general(a, b, (((1,), (0,)), ((), ())), preferred_element_type=F32)


def nt(a, b):
    return lax.dot_general(a, b, (((1,), (1,)), ((), ())), preferred_element_type=F32)


def gelu(x):
    return (0.5 * x) * (1.0 + jnp.tanh(x * (GC + (GC * GA) * (x * x))))


def gelu_slope(x):
    xx = x * x
    t = jnp.tanh(x * (GC + (GC * GA) * xx))
    return 0.5 * (1.0 + t) + (0.5 * x) * (1.0 - t * t) * (GC + (3.0 * GC * GA) * xx)


def kernel(n, codes, stem3, gains, wconv, wpoint, cot, pooled_out, sal_out,
           wc, wp, oh, h0, act0, co0, h1, act1, co1, pool, sendp, recc, cott, grad, ga,
           gc1, gc0, glo, code_l, code_r, pj_l, pj_r, pj_s, stem, r0, r1,
           wl_sem, ws_sem, wr_sem, cs_sem, cr_sem, ps_sem, pr_sem, own_sem,
           hs_sem, hr_sem):
    me = lax.axis_index("seq")
    f = lax.axis_index("fsdp")
    rows = codes.shape[1]
    ch = cot.shape[1]
    half = wpoint.shape[1]
    chan = 2 * half
    prow = rows // POOL
    layers = wpoint.shape[0]
    left, right = me - 1, me + 1
    has_left, has_right = me > 0, me < n - 1
    e0 = D0 + D1

    def local_w():
        copies = []
        for l in range(layers):
            copies.append(pltpu.make_async_copy(wconv.at[l], wc.at[l, :, pl.ds(pl.multiple_of(f * half, half), half), :], wl_sem.at[2 * l]))
            copies.append(pltpu.make_async_copy(wpoint.at[l], wp.at[l, pl.ds(pl.multiple_of(f * half, half), half), :], wl_sem.at[2 * l + 1]))
        return copies

    def remote_w():
        copies = []
        for l in range(layers):
            copies.append(pltpu.make_async_remote_copy(
                wconv.at[l], wc.at[l, :, pl.ds(pl.multiple_of(f * half, half), half), :],
                ws_sem.at[2 * l], wr_sem.at[2 * l], device_id={"fsdp": 1 - f}, device_id_type=MESH))
            copies.append(pltpu.make_async_remote_copy(
                wpoint.at[l], wp.at[l, pl.ds(pl.multiple_of(f * half, half), half), :],
                ws_sem.at[2 * l + 1], wr_sem.at[2 * l + 1], device_id={"fsdp": 1 - f}, device_id_type=MESH))
        return copies

    own_w, sib_w = local_w(), remote_w()
    for c in own_w:
        c.start()

    barrier = pltpu.get_barrier_semaphore()

    @pl.loop(1, n)
    def _(i):
        pl.semaphore_signal(barrier, inc=1, device_id={"seq": lax.rem(me + i, n)}, device_id_type=MESH)

    pl.semaphore_signal(barrier, inc=1, device_id={"fsdp": 1 - f}, device_id_type=MESH)
    for j in range(4):
        quads = [stem3[k].astype(F32) if k < stem3.shape[0] else jnp.zeros((4, chan), F32) for k in range(4 * j, 4 * j + 4)]
        stem[pl.ds(16 * j, 16), :] = jnp.concatenate(quads, axis=0).astype(BF16)
    pl.semaphore_wait(barrier, n)

    def edge(k, to_left_src, to_left_dst, to_right_src, to_right_dst):
        tl = pltpu.make_async_remote_copy(to_left_src, to_left_dst, hs_sem.at[2 * k], hr_sem.at[2 * k],
                                          device_id={"seq": left}, device_id_type=MESH)
        tr = pltpu.make_async_remote_copy(to_right_src, to_right_dst, hs_sem.at[2 * k + 1], hr_sem.at[2 * k + 1],
                                          device_id={"seq": right}, device_id_type=MESH)

        def start():
            pl.when(has_left)(lambda: tl.start())
            pl.when(has_right)(lambda: tr.start())

        def recv():
            pl.when(has_right)(lambda: tl.wait_recv())
            pl.when(has_left)(lambda: tr.wait_recv())

        def sent():
            pl.when(has_left)(lambda: tl.wait_send())
            pl.when(has_right)(lambda: tr.wait_send())

        return start, recv, sent

    codes_x = edge(0, codes.at[:, pl.ds(0, EDGE)], code_r, codes.at[:, pl.ds(rows - EDGE, EDGE)], code_l)
    codes_x[0]()
    sib_w[0].start()
    sib_w[1].start()

    def cot_copy(i, slot):
        peer = lax.rem(me + i, n)
        return pltpu.make_async_remote_copy(
            cot.at[0, :, pl.ds(pl.multiple_of(peer * prow, 128), prow)], recc.at[slot],
            cs_sem.at[i], cr_sem.at[i], device_id={"seq": peer}, device_id_type=MESH)

    cot_own = pltpu.make_async_copy(cot.at[0, :, pl.ds(pl.multiple_of(me * prow, 128), prow)], recc.at[me], own_sem.at[0])
    cot_own.start()

    @pl.loop(1, n)
    def _(i):
        cot_copy(i, me).start()

    sib_w[2].start()
    sib_w[3].start()

    @pl.when(jnp.logical_not(has_left))
    def _():
        code_l[...] = jnp.full(code_l.shape, -1, jnp.int32)
        gc1[pl.ds(0, D1), :] = jnp.zeros((D1, gc1.shape[1]), BF16)
        gc0[pl.ds(0, D0), :] = jnp.zeros((D0, gc0.shape[1]), BF16)
        pj_l[...] = jnp.zeros(pj_l.shape, BF16)

    @pl.when(jnp.logical_not(has_right))
    def _():
        code_r[...] = jnp.full(code_r.shape, -1, jnp.int32)
        gc1[pl.ds(D1 + rows, D1), :] = jnp.zeros((D1, gc1.shape[1]), BF16)
        gc0[pl.ds(D0 + rows, D0), :] = jnp.zeros((D0, gc0.shape[1]), BF16)
        pj_r[...] = jnp.zeros(pj_r.shape, BF16)

    codes_x[1]()

    wide = rows + 2 * EDGE
    ext = jnp.concatenate([code_l[...], codes[...], code_r[...]], axis=1)
    ext = jnp.broadcast_to(ext, (8, wide))
    sub = lax.broadcasted_iota(jnp.int32, (8, wide), 0)
    low_half = sub < 4
    base = jnp.where(low_half, sub, sub - 4)
    groups = []
    off = EDGE - e0 - 7
    for j in range(8):
        a = pltpu.roll(ext, wide - (off + 2 * j), 1)
        b = pltpu.roll(ext, wide - (off + 2 * j + 1), 1)
        groups.append(jnp.where(jnp.where(low_half, a, b) == base, 1.0, 0.0).astype(F32))
    oh[...] = jnp.concatenate(groups, axis=0).T.astype(BF16)

    ext0 = rows + 2 * e0
    hb = ext0 // 4

    @pl.loop(0, 4)
    def _(b):
        s = pl.multiple_of(b * hb, 16)
        h0[pl.ds(s, hb), :] = nn(oh[pl.ds(s, hb), :], stem[...])

    def activate(src, dst, scale, count, halo, layer):
        gain = gains[pl.ds(layer, 1), :]

        @pl.loop(0, count // 16, unroll=2)
        def _(b):
            s = pl.multiple_of(b * 16, 16)
            x = src[pl.ds(s, 16), :]
            pos = me * rows - halo + s + lax.broadcasted_iota(jnp.int32, (16, 1), 0)
            keep = jnp.where((pos >= 0) & (pos < n * rows), 1.0, 0.0)
            r = keep * lax.rsqrt(jnp.sum(x * x, axis=1, keepdims=True) * (1.0 / chan) + 1e-06)
            scale[pl.ds(s, 16), :] = jnp.broadcast_to(r, (16, 128))
            dst[pl.ds(s, 16), :] = gelu(x * r * gain).astype(BF16)

    activate(h0, act0, r0, ext0, e0, 0)

    own_w[0].wait()
    sib_w[0].wait_recv()
    own_w[1].wait()
    sib_w[1].wait_recv()

    def taps(ref, start, count, d, order):
        return jnp.concatenate([ref[pl.ds(pl.multiple_of(start + k * d, 32), count), :] for k in order], axis=1)

    ext1 = rows + 2 * D1
    b1 = ext1 // 2
    flat = (3 * chan, wc.shape[3])

    @pl.loop(0, 2)
    def _(b):
        s = pl.multiple_of(b * b1, 64)
        c = nn(taps(act0, s, b1, D0, (0, 1, 2)), wc[0].reshape(flat))
        co0[pl.ds(s, b1), :] = c
        h1[pl.ds(s, b1), :] = h0[pl.ds(pl.multiple_of(s + D0, 32), b1), :] + nt(gelu(c).astype(BF16), wp[0])

    activate(h1, act1, r1, ext1, D1, 1)

    own_w[2].wait()
    sib_w[2].wait_recv()
    own_w[3].wait()
    sib_w[3].wait_recv()

    b2 = rows // 2
    pb = b2 // POOL
    pr = lax.broadcasted_iota(jnp.int32, (pb, b2), 0)
    pc = lax.broadcasted_iota(jnp.int32, (pb, b2), 1)
    pool_mat = jnp.where((pc == 2 * pr) | (pc == 2 * pr + 1), 0.5, 0.0).astype(BF16)

    @pl.loop(0, 2)
    def _(b):
        s = pl.multiple_of(b * b2, 64)
        c = nn(taps(act1, s, b2, D1, (0, 1, 2)), wc[1].reshape(flat))
        co1[pl.ds(s, b2), :] = c
        h2 = h1[pl.ds(pl.multiple_of(s + D1, 64), b2), :] + nt(gelu(c).astype(BF16), wp[1])
        hi = h2.astype(BF16)
        lo = (h2 - hi.astype(F32)).astype(BF16)
        pool[pl.ds(pl.multiple_of(b * pb, 64), pb), :] = nn(pool_mat, hi) + nn(pool_mat, lo)

    sendp[...] = pool[...].T.reshape(n, ch, prow).astype(BF16)

    def pool_copy(i, slot):
        peer = lax.rem(me + i, n)
        return pltpu.make_async_remote_copy(
            sendp.at[peer], pooled_out.at[0, :, pl.ds(pl.multiple_of(slot * prow, 128), prow)],
            ps_sem.at[i], pr_sem.at[i], device_id={"seq": peer}, device_id_type=MESH)

    pool_own = pltpu.make_async_copy(sendp.at[me], pooled_out.at[0, :, pl.ds(pl.multiple_of(me * prow, 128), prow)], own_sem.at[1])
    pool_own.start()
    cut1, cut2 = 1 + (n - 1) // 4, 1 + 5 * (n - 1) // 8

    def pool_send(first, last):
        @pl.loop(first, last)
        def _(i):
            pool_copy(i, me).start()

    pool_send(1, cut1)

    cot_own.wait()

    @pl.loop(1, n)
    def _(i):
        cot_copy(i, lax.rem(me + n - i, n)).wait_recv()

    cott[...] = recc[...].astype(F32).reshape(chan, prow).astype(BF16)
    er = lax.broadcasted_iota(jnp.int32, (b2, prow), 0)
    ec = lax.broadcasted_iota(jnp.int32, (b2, prow), 1)

    @pl.loop(0, 2)
    def _(b):
        s = pl.multiple_of(b * b2, 64)
        row = er + s
        spread = jnp.where((row == 2 * ec) | (row == 2 * ec + 1), 0.5, 0.0).astype(BF16)
        grad[pl.ds(s, b2), :] = nt(spread, cott[...])

    q = rows // 4
    middle, ends = ((q, 2 * q),), ((0, q), (3 * q, q))

    def get(ref, off, part):
        pieces = [ref[pl.ds(off + s, c), :] for s, c in part]
        return pieces[0] if len(pieces) == 1 else jnp.concatenate(pieces, axis=0)

    def put(ref, off, part, value):
        at = 0
        for s, c in part:
            ref[pl.ds(off + s, c), :] = value[at:at + c]
            at += c

    def conv_grad(gc, d, layer, co, coff, part):
        gb = nn(get(grad, 0, part).astype(BF16), wp[layer])
        put(gc, d, part, (gb * gelu_slope(get(co, coff, part))).astype(BF16))

    def back(gc, d, layer, hidden, scale, hoff, low, part):
        gain = gains[pl.ds(layer, 1), :]
        w = jnp.concatenate([wc[layer, 0], wc[layer, 1], wc[layer, 2]], axis=1)
        lhs = jnp.concatenate([get(gc, k * d, part) for k in (2, 1, 0)], axis=1)
        put(ga, 0, part, nt(lhs, w))
        for first, count in part:
            @pl.loop(0, count // 16, unroll=2)
            def _(b):
                s = pl.multiple_of(first + b * 16, 16)
                h = pl.multiple_of(s + hoff, 16)
                x = hidden[pl.ds(h, 16), :]
                r = scale[pl.ds(h, 16), :][:, 0:1]
                dn = ga[pl.ds(s, 16), :] * gelu_slope(x * r * gain) * gain
                m = jnp.sum(dn * x, axis=1, keepdims=True) * (r * r * r * (1.0 / chan))
                g = grad[pl.ds(s, 16), :] + (dn * r - x * m)
                if low is None:
                    grad[pl.ds(s, 16), :] = g
                else:
                    hi = g.astype(BF16)
                    low[0, pl.ds(s, 16), :] = hi
                    low[1, pl.ds(s, 16), :] = (g - hi.astype(F32)).astype(BF16)

    x1 = edge(1, gc1.at[pl.ds(D1, D1), :], gc1.at[pl.ds(D1 + rows, D1), :],
              gc1.at[pl.ds(rows, D1), :], gc1.at[pl.ds(0, D1), :])
    conv_grad(gc1, D1, 1, co1, 0, ends)
    x1[0]()
    pool_send(cut1, cut2)
    conv_grad(gc1, D1, 1, co1, 0, middle)
    back(gc1, D1, 1, h1, r1, D1, None, middle)
    x1[1]()
    back(gc1, D1, 1, h1, r1, D1, None, ends)

    x0 = edge(2, gc0.at[pl.ds(D0, D0), :], gc0.at[pl.ds(D0 + rows, D0), :],
              gc0.at[pl.ds(rows, D0), :], gc0.at[pl.ds(0, D0), :])
    conv_grad(gc0, D0, 0, co0, D1, ends)
    x0[0]()
    pool_send(cut2, n)
    conv_grad(gc0, D0, 0, co0, D1, middle)
    back(gc0, D0, 0, h0, r0, e0, glo, middle)
    x0[1]()
    back(gc0, D0, 0, h0, r0, e0, glo, ends)

    def project(part):
        return nt(stem[...], get(glo.at[0], 0, part)) + nt(stem[...], get(glo.at[1], 0, part))

    proj_e = project(ends)
    pj_s[0] = proj_e[:, 0:EDGE].astype(BF16)
    pj_s[1] = proj_e[:, q + q - EDGE:q + q].astype(BF16)
    xp = edge(3, pj_s.at[0], pj_r, pj_s.at[1], pj_l)
    xp[0]()
    proj = jnp.concatenate([proj_e[:, 0:q], project(middle), proj_e[:, q:2 * q]], axis=1)
    xp[1]()
    full = jnp.concatenate([pj_l[...].astype(F32), proj, pj_r[...].astype(F32)], axis=1)
    total = jnp.zeros((8, wide), F32)
    for j in range(8):
        grp = full[8 * j:8 * j + 8, :]
        a = pltpu.roll(grp, (2 * j - 7) % wide, 1)
        b = pltpu.roll(grp, (2 * j - 6) % wide, 1)
        total = total + jnp.where(low_half, a, b)
    both = total + pltpu.roll(total, 4, 0)
    sal_out[0] = both[0:4, EDGE:EDGE + rows]

    pool_own.wait()

    @pl.loop(1, n)
    def _(i):
        cot_copy(i, me).wait_send()
        pool_copy(i, lax.rem(me + n - i, n)).wait_recv()
        pool_copy(i, me).wait_send()

    for c in sib_w:
        c.wait_send()
    for x in (codes_x, x1, x0, xp):
        x[2]()


def body(n, base_codes, stem_weight, norm_gains, conv_weight, point_weight, cotangent):
    rows = base_codes.shape[1]
    ch, prow = cotangent.shape[1], rows // POOL
    layers, half, taps_n, ff = conv_weight.shape
    chan = 2 * half
    wconv = conv_weight.transpose(0, 2, 1, 3)
    any_spec = pl.BlockSpec(memory_space=pl.ANY)
    vm = pl.BlockSpec(memory_space=pltpu.VMEM)
    ext0, ext1 = rows + 2 * (D0 + D1), rows + 2 * D1
    V = pltpu.VMEM
    DMA = pltpu.SemaphoreType.DMA
    return pl.pallas_call(
        functools.partial(kernel, n),
        out_shape=(jax.ShapeDtypeStruct(cotangent.shape, BF16),
                   jax.ShapeDtypeStruct((1, 4, rows), F32)),
        in_specs=[vm, vm, vm, any_spec, any_spec, any_spec],
        out_specs=(any_spec, vm),
        scratch_shapes=[
            V((layers, taps_n, chan, ff), BF16), V((layers, chan, ff), BF16),
            V((rows + 2 * EDGE, 64), BF16),
            V((ext0, chan), F32), V((ext0, chan), BF16), V((ext1, ff), F32),
            V((ext1, chan), F32), V((ext1, chan), BF16), V((rows, ff), F32),
            V((prow, chan), F32), V((n, ch, prow), BF16), V((n, ch, prow), BF16),
            V((chan, prow), BF16), V((rows, chan), F32), V((rows, chan), F32),
            V((ext1, ff), BF16), V((rows + 2 * D0, ff), BF16), V((2, rows, chan), BF16),
            V((1, EDGE), jnp.int32), V((1, EDGE), jnp.int32),
            V((64, EDGE), BF16), V((64, EDGE), BF16), V((2, 64, EDGE), BF16),
            V((64, chan), BF16), V((ext0, 128), F32), V((ext1, 128), F32),
            DMA((2 * layers,)), DMA((2 * layers,)), DMA((2 * layers,)),
            DMA((n,)), DMA((n,)), DMA((n,)), DMA((n,)), DMA((2,)),
            DMA((8,)), DMA((8,)),
        ],
        compiler_params=pltpu.CompilerParams(
            collective_id=0, has_side_effects=True, vmem_limit_bytes=56 * 1024 * 1024),
        cost_estimate=pl.CostEstimate(flops=10_000_000_000, bytes_accessed=12_000_000, transcendentals=4_000_000),
    )(base_codes, stem_weight, norm_gains, wconv, point_weight, cotangent)


def solution(mesh):
    in_specs = (
        P(("grp", "fsdp"), "seq"),
        P(),
        P(),
        P(None, "fsdp", None, None),
        P(None, "fsdp", None),
        P(("grp", "fsdp"), "seq", None),
    )
    out_specs = (P(("grp", "fsdp"), "seq", None), P(("grp", "fsdp"), None, "seq"))
    return jax.shard_map(functools.partial(body, mesh.shape["seq"]), mesh=mesh,
                         in_specs=in_specs, out_specs=out_specs, check_vma=False)
```

```python
import functools

import jax
import jax.numpy as jnp
from jax import lax
from jax.experimental import pallas as pl
from jax.experimental.pallas import tpu as pltpu
from jax.sharding import PartitionSpec as P

D0 = 32
D1 = 64
POOL = 2
EDGE = 128
GC = 0.7978845608028654
GA = 0.044715
F32 = jnp.float32
BF16 = jnp.bfloat16
MESH = pl.DeviceIdType.MESH


def nn(a, b):
    return lax.dot_general(a, b, (((1,), (0,)), ((), ())), preferred_element_type=F32)


def nt(a, b):
    return lax.dot_general(a, b, (((1,), (1,)), ((), ())), preferred_element_type=F32)


def gelu(x):
    return (0.5 * x) * (1.0 + jnp.tanh(x * (GC + (GC * GA) * (x * x))))


def gelu_slope(x):
    xx = x * x
    t = jnp.tanh(x * (GC + (GC * GA) * xx))
    return 0.5 * (1.0 + t) + (0.5 * x) * (1.0 - t * t) * (GC + (3.0 * GC * GA) * xx)


def kernel(n, codes, stem3, gains, wconv, wpoint, cot, pooled_out, sal_out,
           wc, wp, oh, h0, act0, co0, h1, act1, co1, pool, sendp, recc, cott, grad, ga,
           gc1, gc0, glo, code_l, code_r, pj_l, pj_r, pj_s, stem, r0, r1,
           wl_sem, ws_sem, wr_sem, cs_sem, cr_sem, ps_sem, pr_sem, own_sem,
           hs_sem, hr_sem):
    me = lax.axis_index("seq")
    f = lax.axis_index("fsdp")
    rows = codes.shape[1]
    ch = cot.shape[1]
    half = wpoint.shape[1]
    chan = 2 * half
    prow = rows // POOL
    layers = wpoint.shape[0]
    left, right = me - 1, me + 1
    has_left, has_right = me > 0, me < n - 1
    e0 = D0 + D1

    def local_w():
        copies = []
        for l in range(layers):
            copies.append(pltpu.make_async_copy(wconv.at[l], wc.at[l, :, pl.ds(pl.multiple_of(f * half, half), half), :], wl_sem.at[2 * l]))
            copies.append(pltpu.make_async_copy(wpoint.at[l], wp.at[l, pl.ds(pl.multiple_of(f * half, half), half), :], wl_sem.at[2 * l + 1]))
        return copies

    def remote_w():
        copies = []
        for l in range(layers):
            copies.append(pltpu.make_async_remote_copy(
                wconv.at[l], wc.at[l, :, pl.ds(pl.multiple_of(f * half, half), half), :],
                ws_sem.at[2 * l], wr_sem.at[2 * l], device_id={"fsdp": 1 - f}, device_id_type=MESH))
            copies.append(pltpu.make_async_remote_copy(
                wpoint.at[l], wp.at[l, pl.ds(pl.multiple_of(f * half, half), half), :],
                ws_sem.at[2 * l + 1], wr_sem.at[2 * l + 1], device_id={"fsdp": 1 - f}, device_id_type=MESH))
        return copies

    own_w, sib_w = local_w(), remote_w()
    for c in own_w:
        c.start()

    barrier = pltpu.get_barrier_semaphore()

    @pl.loop(1, n)
    def _(i):
        pl.semaphore_signal(barrier, inc=1, device_id={"seq": lax.rem(me + i, n)}, device_id_type=MESH)

    pl.semaphore_signal(barrier, inc=1, device_id={"fsdp": 1 - f}, device_id_type=MESH)
    for j in range(4):
        quads = [stem3[k].astype(F32) if k < stem3.shape[0] else jnp.zeros((4, chan), F32) for k in range(4 * j, 4 * j + 4)]
        stem[pl.ds(16 * j, 16), :] = jnp.concatenate(quads, axis=0).astype(BF16)
    pl.semaphore_wait(barrier, n)

    def edge(k, to_left_src, to_left_dst, to_right_src, to_right_dst):
        tl = pltpu.make_async_remote_copy(to_left_src, to_left_dst, hs_sem.at[2 * k], hr_sem.at[2 * k],
                                          device_id={"seq": left}, device_id_type=MESH)
        tr = pltpu.make_async_remote_copy(to_right_src, to_right_dst, hs_sem.at[2 * k + 1], hr_sem.at[2 * k + 1],
                                          device_id={"seq": right}, device_id_type=MESH)

        def start():
            pl.when(has_left)(lambda: tl.start())
            pl.when(has_right)(lambda: tr.start())

        def recv():
            pl.when(has_right)(lambda: tl.wait_recv())
            pl.when(has_left)(lambda: tr.wait_recv())

        def sent():
            pl.when(has_left)(lambda: tl.wait_send())
            pl.when(has_right)(lambda: tr.wait_send())

        return start, recv, sent

    codes_x = edge(0, codes.at[:, pl.ds(0, EDGE)], code_r, codes.at[:, pl.ds(rows - EDGE, EDGE)], code_l)
    codes_x[0]()
    sib_w[0].start()
    sib_w[1].start()

    def cot_copy(i, slot):
        peer = lax.rem(me + i, n)
        return pltpu.make_async_remote_copy(
            cot.at[0, :, pl.ds(pl.multiple_of(peer * prow, 128), prow)], recc.at[slot],
            cs_sem.at[i], cr_sem.at[i], device_id={"seq": peer}, device_id_type=MESH)

    cot_own = pltpu.make_async_copy(cot.at[0, :, pl.ds(pl.multiple_of(me * prow, 128), prow)], recc.at[me], own_sem.at[0])
    cot_own.start()

    @pl.loop(1, n)
    def _(i):
        cot_copy(i, me).start()

    sib_w[2].start()
    sib_w[3].start()

    @pl.when(jnp.logical_not(has_left))
    def _():
        code_l[...] = jnp.full(code_l.shape, -1, jnp.int32)
        gc1[pl.ds(0, D1), :] = jnp.zeros((D1, gc1.shape[1]), BF16)
        gc0[pl.ds(0, D0), :] = jnp.zeros((D0, gc0.shape[1]), BF16)
        pj_l[...] = jnp.zeros(pj_l.shape, BF16)

    @pl.when(jnp.logical_not(has_right))
    def _():
        code_r[...] = jnp.full(code_r.shape, -1, jnp.int32)
        gc1[pl.ds(D1 + rows, D1), :] = jnp.zeros((D1, gc1.shape[1]), BF16)
        gc0[pl.ds(D0 + rows, D0), :] = jnp.zeros((D0, gc0.shape[1]), BF16)
        pj_r[...] = jnp.zeros(pj_r.shape, BF16)

    codes_x[1]()

    wide = rows + 2 * EDGE
    ext = jnp.concatenate([code_l[...], codes[...], code_r[...]], axis=1)
    ext = jnp.broadcast_to(ext, (8, wide))
    sub = lax.broadcasted_iota(jnp.int32, (8, wide), 0)
    low_half = sub < 4
    base = jnp.where(low_half, sub, sub - 4)
    groups = []
    off = EDGE - e0 - 7
    for j in range(8):
        a = pltpu.roll(ext, wide - (off + 2 * j), 1)
        b = pltpu.roll(ext, wide - (off + 2 * j + 1), 1)
        groups.append(jnp.where(jnp.where(low_half, a, b) == base, 1.0, 0.0).astype(F32))
    oh[...] = jnp.concatenate(groups, axis=0).T.astype(BF16)

    ext0 = rows + 2 * e0
    hb = ext0 // 4

    @pl.loop(0, 4)
    def _(b):
        s = pl.multiple_of(b * hb, 16)
        h0[pl.ds(s, hb), :] = nn(oh[pl.ds(s, hb), :], stem[...])

    def activate(src, dst, scale, count, halo, layer):
        gain = gains[pl.ds(layer, 1), :]

        @pl.loop(0, count // 16, unroll=8)
        def _(b):
            s = pl.multiple_of(b * 16, 16)
            x = src[pl.ds(s, 16), :]
            pos = me * rows - halo + s + lax.broadcasted_iota(jnp.int32, (16, 1), 0)
            keep = jnp.where((pos >= 0) & (pos < n * rows), 1.0, 0.0)
            r = keep * lax.rsqrt(jnp.sum(x * x, axis=1, keepdims=True) * (1.0 / chan) + 1e-06)
            scale[pl.ds(s, 16), :] = jnp.broadcast_to(r, (16, 128))
            dst[pl.ds(s, 16), :] = gelu(x * r * gain).astype(BF16)

    activate(h0, act0, r0, ext0, e0, 0)

    own_w[0].wait()
    sib_w[0].wait_recv()
    own_w[1].wait()
    sib_w[1].wait_recv()

    def taps(ref, start, count, d, order):
        return jnp.concatenate([ref[pl.ds(pl.multiple_of(start + k * d, 32), count), :] for k in order], axis=1)

    ext1 = rows + 2 * D1
    b1 = ext1 // 2
    flat = (3 * chan, wc.shape[3])

    @pl.loop(0, 2)
    def _(b):
        s = pl.multiple_of(b * b1, 64)
        c = nn(taps(act0, s, b1, D0, (0, 1, 2)), wc[0].reshape(flat))
        co0[pl.ds(s, b1), :] = c
        h1[pl.ds(s, b1), :] = h0[pl.ds(pl.multiple_of(s + D0, 32), b1), :] + nt(gelu(c).astype(BF16), wp[0])

    activate(h1, act1, r1, ext1, D1, 1)

    own_w[2].wait()
    sib_w[2].wait_recv()
    own_w[3].wait()
    sib_w[3].wait_recv()

    b2 = rows // 2
    pb = b2 // POOL
    pr = lax.broadcasted_iota(jnp.int32, (pb, b2), 0)
    pc = lax.broadcasted_iota(jnp.int32, (pb, b2), 1)
    pool_mat = jnp.where((pc == 2 * pr) | (pc == 2 * pr + 1), 0.5, 0.0).astype(BF16)

    @pl.loop(0, 2)
    def _(b):
        s = pl.multiple_of(b * b2, 64)
        c = nn(taps(act1, s, b2, D1, (0, 1, 2)), wc[1].reshape(flat))
        co1[pl.ds(s, b2), :] = c
        h2 = h1[pl.ds(pl.multiple_of(s + D1, 64), b2), :] + nt(gelu(c).astype(BF16), wp[1])
        hi = h2.astype(BF16)
        lo = (h2 - hi.astype(F32)).astype(BF16)
        pool[pl.ds(pl.multiple_of(b * pb, 64), pb), :] = nn(pool_mat, hi) + nn(pool_mat, lo)

    sendp[...] = pool[...].T.reshape(n, ch, prow).astype(BF16)

    def pool_copy(i, slot):
        peer = lax.rem(me + i, n)
        return pltpu.make_async_remote_copy(
            sendp.at[peer], pooled_out.at[0, :, pl.ds(pl.multiple_of(slot * prow, 128), prow)],
            ps_sem.at[i], pr_sem.at[i], device_id={"seq": peer}, device_id_type=MESH)

    pool_own = pltpu.make_async_copy(sendp.at[me], pooled_out.at[0, :, pl.ds(pl.multiple_of(me * prow, 128), prow)], own_sem.at[1])
    pool_own.start()
    cut1, cut2 = 1 + (n - 1) // 4, 1 + 5 * (n - 1) // 8

    def pool_send(first, last):
        @pl.loop(first, last)
        def _(i):
            pool_copy(i, me).start()

    pool_send(1, cut1)

    cot_own.wait()

    @pl.loop(1, n)
    def _(i):
        cot_copy(i, lax.rem(me + n - i, n)).wait_recv()

    cott[...] = recc[...].astype(F32).reshape(chan, prow).astype(BF16)
    er = lax.broadcasted_iota(jnp.int32, (b2, prow), 0)
    ec = lax.broadcasted_iota(jnp.int32, (b2, prow), 1)

    @pl.loop(0, 2)
    def _(b):
        s = pl.multiple_of(b * b2, 64)
        row = er + s
        spread = jnp.where((row == 2 * ec) | (row == 2 * ec + 1), 0.5, 0.0).astype(BF16)
        grad[pl.ds(s, b2), :] = nt(spread, cott[...])

    q = rows // 4
    middle, ends = ((q, 2 * q),), ((0, q), (3 * q, q))

    def get(ref, off, part):
        pieces = [ref[pl.ds(off + s, c), :] for s, c in part]
        return pieces[0] if len(pieces) == 1 else jnp.concatenate(pieces, axis=0)

    def put(ref, off, part, value):
        at = 0
        for s, c in part:
            ref[pl.ds(off + s, c), :] = value[at:at + c]
            at += c

    def conv_grad(gc, d, layer, co, coff, part):
        gb = nn(get(grad, 0, part).astype(BF16), wp[layer])
        put(gc, d, part, (gb * gelu_slope(get(co, coff, part))).astype(BF16))

    def back(gc, d, layer, hidden, scale, hoff, low, part):
        gain = gains[pl.ds(layer, 1), :]
        w = jnp.concatenate([wc[layer, 0], wc[layer, 1], wc[layer, 2]], axis=1)
        lhs = jnp.concatenate([get(gc, k * d, part) for k in (2, 1, 0)], axis=1)
        put(ga, 0, part, nt(lhs, w))
        for first, count in part:
            @pl.loop(0, count // 16, unroll=8)
            def _(b):
                s = pl.multiple_of(first + b * 16, 16)
                h = pl.multiple_of(s + hoff, 16)
                x = hidden[pl.ds(h, 16), :]
                r = scale[pl.ds(h, 16), :][:, 0:1]
                dn = ga[pl.ds(s, 16), :] * gelu_slope(x * r * gain) * gain
                m = jnp.sum(dn * x, axis=1, keepdims=True) * (r * r * r * (1.0 / chan))
                g = grad[pl.ds(s, 16), :] + (dn * r - x * m)
                if low is None:
                    grad[pl.ds(s, 16), :] = g
                else:
                    hi = g.astype(BF16)
                    low[0, pl.ds(s, 16), :] = hi
                    low[1, pl.ds(s, 16), :] = (g - hi.astype(F32)).astype(BF16)

    x1 = edge(1, gc1.at[pl.ds(D1, D1), :], gc1.at[pl.ds(D1 + rows, D1), :],
              gc1.at[pl.ds(rows, D1), :], gc1.at[pl.ds(0, D1), :])
    conv_grad(gc1, D1, 1, co1, 0, ends)
    x1[0]()
    pool_send(cut1, cut2)
    conv_grad(gc1, D1, 1, co1, 0, middle)
    back(gc1, D1, 1, h1, r1, D1, None, middle)
    x1[1]()
    back(gc1, D1, 1, h1, r1, D1, None, ends)

    x0 = edge(2, gc0.at[pl.ds(D0, D0), :], gc0.at[pl.ds(D0 + rows, D0), :],
              gc0.at[pl.ds(rows, D0), :], gc0.at[pl.ds(0, D0), :])
    conv_grad(gc0, D0, 0, co0, D1, ends)
    x0[0]()
    pool_send(cut2, n)
    conv_grad(gc0, D0, 0, co0, D1, middle)
    back(gc0, D0, 0, h0, r0, e0, glo, middle)
    x0[1]()
    back(gc0, D0, 0, h0, r0, e0, glo, ends)

    def project(part):
        return nt(stem[...], get(glo.at[0], 0, part)) + nt(stem[...], get(glo.at[1], 0, part))

    proj_e = project(ends)
    pj_s[0] = proj_e[:, 0:EDGE].astype(BF16)
    pj_s[1] = proj_e[:, q + q - EDGE:q + q].astype(BF16)
    xp = edge(3, pj_s.at[0], pj_r, pj_s.at[1], pj_l)
    xp[0]()
    proj = jnp.concatenate([proj_e[:, 0:q], project(middle), proj_e[:, q:2 * q]], axis=1)
    xp[1]()
    full = jnp.concatenate([pj_l[...].astype(F32), proj, pj_r[...].astype(F32)], axis=1)
    total = jnp.zeros((8, wide), F32)
    for j in range(8):
        grp = full[8 * j:8 * j + 8, :]
        a = pltpu.roll(grp, (2 * j - 7) % wide, 1)
        b = pltpu.roll(grp, (2 * j - 6) % wide, 1)
        total = total + jnp.where(low_half, a, b)
    both = total + pltpu.roll(total, 4, 0)
    sal_out[0] = both[0:4, EDGE:EDGE + rows]

    pool_own.wait()

    @pl.loop(1, n)
    def _(i):
        cot_copy(i, me).wait_send()
        pool_copy(i, lax.rem(me + n - i, n)).wait_recv()
        pool_copy(i, me).wait_send()

    for c in sib_w:
        c.wait_send()
    for x in (codes_x, x1, x0, xp):
        x[2]()


def body(n, base_codes, stem_weight, norm_gains, conv_weight, point_weight, cotangent):
    rows = base_codes.shape[1]
    ch, prow = cotangent.shape[1], rows // POOL
    layers, half, taps_n, ff = conv_weight.shape
    chan = 2 * half
    wconv = conv_weight.transpose(0, 2, 1, 3)
    any_spec = pl.BlockSpec(memory_space=pl.ANY)
    vm = pl.BlockSpec(memory_space=pltpu.VMEM)
    ext0, ext1 = rows + 2 * (D0 + D1), rows + 2 * D1
    V = pltpu.VMEM
    DMA = pltpu.SemaphoreType.DMA
    return pl.pallas_call(
        functools.partial(kernel, n),
        out_shape=(jax.ShapeDtypeStruct(cotangent.shape, BF16),
                   jax.ShapeDtypeStruct((1, 4, rows), F32)),
        in_specs=[vm, vm, vm, any_spec, any_spec, any_spec],
        out_specs=(any_spec, vm),
        scratch_shapes=[
            V((layers, taps_n, chan, ff), BF16), V((layers, chan, ff), BF16),
            V((rows + 2 * EDGE, 64), BF16),
            V((ext0, chan), F32), V((ext0, chan), BF16), V((ext1, ff), F32),
            V((ext1, chan), F32), V((ext1, chan), BF16), V((rows, ff), F32),
            V((prow, chan), F32), V((n, ch, prow), BF16), V((n, ch, prow), BF16),
            V((chan, prow), BF16), V((rows, chan), F32), V((rows, chan), F32),
            V((ext1, ff), BF16), V((rows + 2 * D0, ff), BF16), V((2, rows, chan), BF16),
            V((1, EDGE), jnp.int32), V((1, EDGE), jnp.int32),
            V((64, EDGE), BF16), V((64, EDGE), BF16), V((2, 64, EDGE), BF16),
            V((64, chan), BF16), V((ext0, 128), F32), V((ext1, 128), F32),
            DMA((2 * layers,)), DMA((2 * layers,)), DMA((2 * layers,)),
            DMA((n,)), DMA((n,)), DMA((n,)), DMA((n,)), DMA((2,)),
            DMA((8,)), DMA((8,)),
        ],
        compiler_params=pltpu.CompilerParams(
            collective_id=0, has_side_effects=True, vmem_limit_bytes=56 * 1024 * 1024),
        cost_estimate=pl.CostEstimate(flops=10_000_000_000, bytes_accessed=12_000_000, transcendentals=4_000_000),
    )(base_codes, stem_weight, norm_gains, wconv, point_weight, cotangent)


def solution(mesh):
    in_specs = (
        P(("grp", "fsdp"), "seq"),
        P(),
        P(),
        P(None, "fsdp", None, None),
        P(None, "fsdp", None),
        P(("grp", "fsdp"), "seq", None),
    )
    out_specs = (P(("grp", "fsdp"), "seq", None), P(("grp", "fsdp"), None, "seq"))
    return jax.shard_map(functools.partial(body, mesh.shape["seq"]), mesh=mesh,
                         in_specs=in_specs, out_specs=out_specs, check_vma=False)
```
